32 devices in a mesh: ctx: 16 (over z, y, x), head: 2 (over core).
Axes of the slice: x: 2, y: 2, z: 4, core: 2. Of those that a mesh axis runs over, the one named last changes fastest.
Arguments:
- queries: bfloat16 [2048, 4096], P('ctx', 'head'), may hold values from -30 to 30
- keys: bfloat16 [8, 2048, 1024], P(None, 'ctx', 'head'), may hold values from -12 to 12
- values: bfloat16 [8, 2048, 1024], P(None, 'ctx', 'head'), may hold values from -6 to 6
- out_weight: bfloat16 [4096, 4096], P('head'), may hold values from -0.09375 to 0.09375
- vertical: int32 [8, 8], P('head'), may hold values from 0 to 111, as said below
- slash: int32 [8, 8], P('head'), may hold values from 1 to 112, as said below
Outputs:
- mixed: bfloat16 [2048, 4096], P('ctx', 'head')
The draws below stay inside these ranges and needn't reach their ends.
Inputs may be any that keep to these rules, and one draw needn't show every extreme that they name: `vertical`: for each key-value head the 8 entries have distinct residues modulo 16, and all lie before block (7) * 16. `slash`: for each key-value head the 8 offsets have distinct residues modulo 16.
All inputs are finite; a program needn't handle non-finite values.
Results may differ from the reference program's by a relative error of at most 0.02.
Values may be sent and summed in bfloat16 or wider, within the bound.
A program may use at most 128 MiB of HBM per device.

```python
import jax
import jax.numpy as jnp
from jax import lax

H = 32
KVH = 8
HD = 128
D = 4096
BLK = 128
NB_DEV = 8
QTOK = 2048
NV = 8
NS = 8
N_CTX = 16


def draw_queries(key, part):
    key = jax.random.fold_in(key, 3)
    first = jax.random.fold_in(key, 0)
    base = jnp.clip(jax.random.normal(first, (QTOK, H * HD), jnp.float32), -6.0, 6.0)
    return base.astype(jnp.bfloat16)


def draw_keys(key, part):
    key = jax.random.fold_in(key, 4)
    first = jax.random.fold_in(key, 0)
    shape = (NB_DEV, N_CTX * BLK, KVH * HD)
    base = jnp.clip(jax.random.normal(first, shape, jnp.float32), -6.0, 6.0)
    return base.astype(jnp.bfloat16)


def draw_vertical(key, part):
    key = jax.random.fold_in(key, 5)

    def one_head(subkey):
        left, right = jax.random.split(subkey)
        residues = jax.random.permutation(left, N_CTX)[:NV]
        rounds = jax.random.randint(right, (NV,), 0, NB_DEV - 1)
        return (residues + N_CTX * rounds).astype(jnp.int32)
    return jax.vmap(one_head)(jax.random.split(key, KVH))


def draw_slash(key, part):
    key = jax.random.fold_in(key, 6)

    def one_head(subkey):
        left, middle, right = jax.random.split(subkey, 3)
        residues = jax.random.permutation(left, N_CTX)[:NS]
        rounds = jnp.minimum(jax.random.randint(middle, (NS,), 0, NB_DEV - 1), jax.random.randint(right, (NS,), 0, NB_DEV - 1))
        offsets = residues + N_CTX * rounds
        offsets = jnp.where(offsets == 0, N_CTX * (NB_DEV - 1), offsets)
        return offsets.astype(jnp.int32)
    return jax.vmap(one_head)(jax.random.split(key, KVH))


def levels(key, extent, shards, low, top_value):
    def one(axis_at, blocks):
        draws = jax.random.uniform(jax.random.fold_in(jax.random.fold_in(key, 6), axis_at), (blocks,), jnp.float32, low / len(shards), top_value / len(shards))
        return jnp.repeat(jnp.exp(draws), extent[axis_at] // blocks).reshape((-1,) + (1,) * (len(extent) - axis_at - 1))

    loudness = one(*shards[0])
    for cut in shards[1:]:
        loudness = loudness * one(*cut)
    return loudness


def gaussian(key, dims, spread, most, cuts=(), kind=jnp.bfloat16):
    entries = spread * jax.random.normal(key, dims, jnp.float32)
    if cuts:
        entries = entries * levels(key, dims, cuts, -0.22, 0.18)
    return jnp.clip(entries, -most, most).astype(kind)


def setup_inputs(seed: int = 0) -> dict:
    key_of = jax.random.split(jax.random.key(seed), 7)
    return {
        "queries": draw_queries(jax.random.fold_in(key_of[6], 71), 0),
        "keys": draw_keys(jax.random.fold_in(key_of[6], 71), 0),
        "values": gaussian(key_of[2], (NB_DEV, N_CTX * BLK, KVH * HD), 1.0, 6.0, ((1, 16), (2, 2))),
        "out_weight": gaussian(key_of[3], (H * HD, D), (H * HD) ** -0.5, 0.09375, ((0, 2),)),
        "vertical": draw_vertical(jax.random.fold_in(key_of[6], 71), 0),
        "slash": draw_slash(jax.random.fold_in(key_of[6], 71), 0),
    }


def reference(queries, keys, values, out_weight, vertical, slash):
    blocks = NB_DEV * N_CTX
    heads_per = H // KVH
    factor = HD ** -0.5
    key_blocks = keys.reshape(blocks, BLK, KVH, HD)
    value_blocks = values.reshape(blocks, BLK, KVH, HD)
    causal = jnp.arange(BLK)[:, None] >= jnp.arange(BLK)[None, :]
    tiles = NV + NS + 1
    last_tile = jnp.arange(tiles) == tiles - 1

    def one_block(qblock):
        own_block = (NB_DEV - 1) * N_CTX + qblock
        query_tile = lax.dynamic_slice_in_dim(queries, qblock * BLK, BLK, 0)
        query_tile = query_tile.reshape(BLK, KVH, heads_per, HD).astype(jnp.float32)
        results = []
        for kv_head in range(KVH):
            slash_blocks = own_block - slash[kv_head]
            repeated = jnp.any(slash_blocks[:, None] == vertical[kv_head][None, :], axis=1)
            chosen = jnp.concatenate([vertical[kv_head].astype(jnp.int32), slash_blocks.astype(jnp.int32), jnp.reshape(own_block, (1,)).astype(jnp.int32)])
            valid = jnp.concatenate([jnp.ones((NV,), jnp.bool_), jnp.logical_not(repeated), jnp.ones((1,), jnp.bool_)])
            tile_keys = jnp.take(key_blocks[:, :, kv_head, :], chosen, axis=0).astype(jnp.float32)
            tile_values = jnp.take(value_blocks[:, :, kv_head, :], chosen, axis=0).astype(jnp.float32)
            allowed = valid[None, :, None] & (causal[:, None, :] | jnp.logical_not(last_tile)[None, :, None])
            scores = jnp.einsum("qgd,tkd->gqtk", query_tile[:, kv_head], tile_keys) * factor
            scores = jnp.where(allowed[None], scores, -jnp.inf)
            peak = jnp.max(scores, axis=(2, 3), keepdims=True)
            weights = jnp.exp(scores - peak)
            total = jnp.sum(weights, axis=(2, 3))
            rounded = lax.optimization_barrier(weights.astype(jnp.bfloat16)).astype(jnp.float32)
            summed = jnp.einsum("gqtk,tkd->gqd", rounded, tile_values)
            results.append(jnp.transpose(summed / total[:, :, None], (1, 0, 2)))
        return jnp.stack(results, axis=1).reshape(BLK, H * HD).astype(jnp.bfloat16)

    attended = lax.map(one_block, jnp.arange(N_CTX, dtype=jnp.int32)).reshape(QTOK, H * HD)
    return jnp.dot(attended, out_weight, preferred_element_type=jnp.float32).astype(jnp.bfloat16)
```

```python
import functools
import math

import jax
import jax.numpy as jnp
import numpy as np
from jax import lax
from jax.experimental import pallas as pl
from jax.experimental.pallas import tpu as pltpu
from jax.sharding import PartitionSpec as P

H = 32
KVH = 8
HD = 128
NEGATIVE = -1e30
SCALE = HD ** (-0.5) * math.log2(math.e)
MESH = pl.DeviceIdType.MESH


def send_order(shards):
    high = list(range(shards // 2, shards))
    low = list(range(1, shards // 2))
    order = [0]
    for place in range(shards // 2):
        order.append(high[place])
        if place < len(low):
            order.append(low[place])
    steps = shards.bit_length() - 1
    weights = np.cumsum(np.arange(2, steps + 2))
    ends = np.floor((shards - 1) * weights / (weights[-1] + 1)).astype(int)
    ends[-1] = shards - 1
    bounds = [1] + [int(end) + 1 for end in ends]
    return order, bounds


def gather_bits(shards, swap):
    bits = [1 << place for place in reversed(range(shards.bit_length() - 1))]
    if swap:
        bits[-1], bits[-2] = bits[-2], bits[-1]
    return bits


def flipped(index, offset):
    bit = 1
    result = index
    while bit <= offset:
        if offset & bit:
            result = result + bit * (1 - 2 * ((index // bit) % 2))
        bit *= 2
    return result


def kernel(
    shards, heads, index_ref, bias_ref, q_ref, k_ref, v_ref, w_hbm, out_ref,
    qt, acc, top, total, send, recv, vert_k, vert_v, weight, att, part, part_in,
    send_sem, recv_sem, vs_send, vs_recv, w_sem, h_send, h_recv,
):
    groups = qt.shape[0]
    rounds, block = k_ref.shape[0], k_ref.shape[1]
    per = q_ref.shape[1] // (groups * HD)
    width = out_ref.shape[1]
    tile = part.shape[3]
    tiles = width // tile
    me = lax.axis_index("ctx")
    head = lax.axis_index("head")
    order, bounds = send_order(shards)
    steps = shards.bit_length() - 1
    bits_k, bits_v = gather_bits(shards, False), gather_bits(shards, True)

    w_copy = pltpu.make_async_copy(w_hbm, weight, w_sem)
    w_copy.start()

    barrier = pltpu.get_barrier_semaphore()
    for offset in range(1, shards):
        pl.semaphore_signal(
            barrier, inc=1, device_id=(flipped(me, offset), head), device_id_type=MESH
        )
    for offset in range(1, heads):
        pl.semaphore_signal(
            barrier, inc=1, device_id=(me, lax.rem(head + offset, heads)), device_id_type=MESH
        )

    def gather_copy(step, which):
        buffer = (vert_k, vert_v)[which]
        bit = (bits_k, bits_v)[which][step]
        size = 1 << step
        return pltpu.make_async_remote_copy(
            src_ref=buffer.at[pl.ds(0, size)],
            dst_ref=buffer.at[pl.ds(size, size)],
            send_sem=vs_send.at[step, which],
            recv_sem=vs_recv.at[step, which],
            device_id=(flipped(me, bit), head),
            device_id_type=MESH,
        )

    def slash_copy(place, offset):
        return pltpu.make_async_remote_copy(
            src_ref=send.at[place],
            dst_ref=recv.at[place],
            send_sem=send_sem.at[place],
            recv_sem=recv_sem.at[place],
            device_id=(flipped(me, offset), head),
            device_id_type=MESH,
        )

    def fill(target, place):
        for group in range(groups):
            at = index_ref[group, place]
            columns = slice(group * HD, (group + 1) * HD)
            target[place, group, 0] = k_ref[at, :, columns]
            target[place, group, 1] = v_ref[at, :, columns]

    def start_wave(wave):
        for place in range(bounds[wave], bounds[wave + 1]):
            slash_copy(place, order[place]).start()

    for group in range(groups):
        at = index_ref[group, shards]
        columns = slice(group * HD, (group + 1) * HD)
        vert_k[0, group] = k_ref[at, :, columns]
        vert_v[0, group] = v_ref[at, :, columns]

    pl.semaphore_wait(barrier, shards - 1 + heads - 1)
    for which in range(2):
        gather_copy(0, which).start()

    def fill_send(place, carry):
        fill(send, place)
        return carry

    lax.fori_loop(bounds[0], bounds[1], fill_send, 0)
    start_wave(0)
    lax.fori_loop(bounds[1], shards, fill_send, 0)
    fill(recv, 0)

    for group in range(groups):
        for one in range(per):
            start = (group * per + one) * HD
            rows = q_ref[:, start : start + HD].astype(jnp.float32)
            qt[group, :, one * block : (one + 1) * block] = rows.T.astype(jnp.bfloat16)

    columns_q = per * block
    causal = (
        lax.broadcasted_iota(jnp.int32, (block, columns_q), 0)
        <= lax.broadcasted_iota(jnp.int32, (block, columns_q), 1) % block
    )

    def weigh(values_tile, weights):
        return lax.dot_general(
            values_tile,
            weights.astype(jnp.bfloat16),
            (((0,), (0,)), ((), ())),
            preferred_element_type=jnp.float32,
        )

    for group in range(groups):
        columns = slice(group * HD, (group + 1) * HD)
        scores = (
            jnp.dot(
                k_ref[rounds - 1, :, columns], qt[group], preferred_element_type=jnp.float32
            )
            * SCALE
        )
        scores = jnp.where(causal, scores, NEGATIVE)
        peak = jnp.max(scores, axis=0, keepdims=True)
        weights = jnp.exp2(scores - peak)
        top[group] = peak
        total[group] = jnp.sum(weights, axis=0, keepdims=True)
        acc[group] = weigh(v_ref[rounds - 1, :, columns], weights)

    def absorb(group, keys_tile, values_tile, bias):
        scores = (
            jnp.dot(keys_tile, qt[group], preferred_element_type=jnp.float32) * SCALE + bias
        )
        before = top[group]
        peak = jnp.maximum(before, jnp.max(scores, axis=0, keepdims=True))
        weights = jnp.exp2(scores - peak)
        shrink = jnp.exp2(before - peak)
        top[group] = peak
        total[group] = total[group] * shrink + jnp.sum(weights, axis=0, keepdims=True)
        acc[group] = acc[group] * shrink + weigh(values_tile, weights)

    def absorb_vertical(low, high, shift):
        def body(at, carry):
            place, group = low + at // groups, at % groups
            absorb(
                group,
                vert_k[place, group],
                vert_v[place + shift, group],
                bias_ref[group, place],
            )
            return carry

        lax.fori_loop(0, (high - low) * groups, body, 0)

    def absorb_slash_at(place):
        def body(group, carry):
            absorb(
                group, recv[place, group, 0], recv[place, group, 1], bias_ref[group, shards + place]
            )
            return carry

        lax.fori_loop(0, groups, body, 0)

    def absorb_wave(wave):
        def body(place, carry):
            slash_copy(place, 1).wait_recv()
            absorb_slash_at(place)
            return carry

        lax.fori_loop(bounds[wave], bounds[wave + 1], body, 0)

    absorb_slash_at(0)
    absorb_vertical(0, 1, 0)
    quarter = shards // 4
    for step in range(steps):
        for which in range(2):
            gather_copy(step, which).wait_recv()
        if step < steps - 1:
            for which in range(2):
                gather_copy(step + 1, which).start()
            start_wave(step + 1)
        if step < steps - 2:
            absorb_vertical(1 << step, 2 << step, 0)
        if step == steps - 1:
            absorb_vertical(quarter, 2 * quarter, quarter)
            absorb_vertical(2 * quarter, 3 * quarter, -quarter)
            absorb_vertical(3 * quarter, 4 * quarter, 0)
        if step >= 1:
            absorb_wave(step - 1)
    absorb_wave(steps - 1)

    for group in range(groups):
        for one in range(per):
            columns = slice(one * block, (one + 1) * block)
            scaled = acc[group, :, columns] / total[group, :, columns]
            start = (group * per + one) * HD
            att[:, start : start + HD] = scaled.T.astype(jnp.bfloat16)
    w_copy.wait()

    def project(owner, at):
        start = pl.multiple_of(owner * width + at * tile, tile)
        return jnp.dot(
            att[...], weight[:, pl.ds(start, tile)], preferred_element_type=jnp.float32
        )

    def head_copy(offset, at):
        return pltpu.make_async_remote_copy(
            src_ref=part.at[offset - 1, at],
            dst_ref=part_in.at[offset - 1, at],
            send_sem=h_send.at[offset - 1, at],
            recv_sem=h_recv.at[offset - 1, at],
            device_id=(me, lax.rem(head + offset, heads)),
            device_id_type=MESH,
        )

    for offset in range(1, heads):

        def give(at, carry, offset=offset):
            part[offset - 1, at] = project(lax.rem(head + offset, heads), at).astype(jnp.bfloat16)
            head_copy(offset, at).start()
            return carry

        lax.fori_loop(0, tiles, give, 0)

    def keep(at, carry):
        result = project(head, at)
        for offset in range(1, heads):
            head_copy(offset, at).wait_recv()
            result = result + part_in[offset - 1, at].astype(jnp.float32)
        start = pl.multiple_of(at * tile, tile)
        out_ref[:, pl.ds(start, tile)] = result.astype(jnp.bfloat16)
        return carry

    lax.fori_loop(0, tiles, keep, 0)

    for step in range(steps):
        for which in range(2):
            gather_copy(step, which).wait_send()

    def sent(place, carry):
        slash_copy(place, 1).wait_send()
        return carry

    lax.fori_loop(1, shards, sent, 0)
    for offset in range(1, heads):
        for at in range(tiles):
            head_copy(offset, at).wait_send()


def per_device(shards, heads, queries, keys, values, out_weight, vertical, slash):
    me = lax.axis_index("ctx")
    groups = vertical.shape[0]
    rounds = keys.shape[0]
    block = queries.shape[0]
    per = H // KVH
    width = out_weight.shape[1] // heads
    tile = min(512, width)
    last_base = (rounds - 1) * shards

    order, _ = send_order(shards)
    partner = me ^ jnp.asarray(order, jnp.int32)
    residue_s = slash % shards
    wanted = (partner - me) % shards
    matching = residue_s[:, None, :] == wanted[None, :, None]
    chosen = jnp.sum(jnp.where(matching, slash[:, None, :], 0), axis=2)
    slash_round = (last_base + partner[None, :] - chosen) // shards
    holding = vertical % shards == me
    vertical_round = jnp.sum(jnp.where(holding, vertical // shards, 0), axis=1)
    index = jnp.concatenate([slash_round, vertical_round[:, None]], axis=1).astype(jnp.int32)

    bits = gather_bits(shards, False)
    flips = [sum(b for i, b in enumerate(bits) if (p >> i) & 1) for p in range(shards)]
    source = me ^ jnp.asarray(flips, jnp.int32)
    has_vertical = jnp.any((vertical % shards)[:, None, :] == source[None, :, None], axis=2)
    back = (me - partner) % shards
    slash_blocks = last_base + me - slash
    repeated = jnp.any(slash_blocks[:, :, None] == vertical[:, None, :], axis=2)
    has_slash = jnp.any(
        (residue_s[:, None, :] == back[None, :, None]) & ~repeated[:, None, :], axis=2
    )
    bias = jnp.where(
        jnp.concatenate([has_vertical, has_slash], axis=1), 0.0, NEGATIVE
    ).astype(jnp.float32)

    steps = shards.bit_length() - 1
    smem = pl.BlockSpec(memory_space=pltpu.SMEM)
    vmem = pl.BlockSpec(memory_space=pltpu.VMEM)
    dma = pltpu.SemaphoreType.DMA
    return pl.pallas_call(
        functools.partial(kernel, shards, heads),
        out_shape=jax.ShapeDtypeStruct((block, width), jnp.bfloat16),
        in_specs=[smem, smem, vmem, vmem, vmem, pl.BlockSpec(memory_space=pl.ANY)],
        out_specs=vmem,
        scratch_shapes=[
            pltpu.VMEM((groups, HD, per * block), jnp.bfloat16),
            pltpu.VMEM((groups, HD, per * block), jnp.float32),
            pltpu.VMEM((groups, 1, per * block), jnp.float32),
            pltpu.VMEM((groups, 1, per * block), jnp.float32),
            pltpu.VMEM((shards, groups, 2, block, HD), jnp.bfloat16),
            pltpu.VMEM((shards, groups, 2, block, HD), jnp.bfloat16),
            pltpu.VMEM((shards, groups, block, HD), jnp.bfloat16),
            pltpu.VMEM((shards, groups, block, HD), jnp.bfloat16),
            pltpu.VMEM(out_weight.shape, jnp.bfloat16),
            pltpu.VMEM((block, groups * per * HD), jnp.bfloat16),
            pltpu.VMEM((heads - 1, width // tile, block, tile), jnp.bfloat16),
            pltpu.VMEM((heads - 1, width // tile, block, tile), jnp.bfloat16),
            dma((shards,)),
            dma((shards,)),
            dma((steps, 2)),
            dma((steps, 2)),
            dma,
            dma((heads - 1, width // tile)),
            dma((heads - 1, width // tile)),
        ],
        compiler_params=pltpu.CompilerParams(
            collective_id=0, has_side_effects=True, vmem_limit_bytes=56 * 1024 * 1024
        ),
    )(index, bias, queries, keys, values, out_weight)


def solution(mesh):
    in_specs = (
        P("ctx", "head"),
        P(None, "ctx", "head"),
        P(None, "ctx", "head"),
        P("head", None),
        P("head", None),
        P("head", None),
    )
    return jax.shard_map(
        functools.partial(per_device, mesh.shape["ctx"], mesh.shape["head"]),
        mesh=mesh,
        in_specs=in_specs,
        out_specs=P("ctx", "head"),
        check_vma=False,
    )
```

```python
import functools
import math

import jax
import jax.numpy as jnp
from jax import lax
from jax.experimental import pallas as pl
from jax.experimental.pallas import tpu as pltpu
from jax.sharding import PartitionSpec as P

H = 32
KVH = 8
HD = 128
NEGATIVE = -1e30
SCALE = HD ** (-0.5) * math.log2(math.e)
MESH = pl.DeviceIdType.MESH


PACE = 1.5
TOGETHER = 2


def send_offset(shards, place):
    return place // 2 + (place % 2) * (shards // 2)


def gather_bits(shards, swap):
    bits = [1 << place for place in reversed(range(shards.bit_length() - 1))]
    if swap:
        bits[-1], bits[-2] = bits[-2], bits[-1]
    return bits


def flipped(shards, index, offset):
    result = index
    for bit in (1 << place for place in range(shards.bit_length() - 1)):
        result = result + bit * ((offset // bit) % 2) * (1 - 2 * ((index // bit) % 2))
    return result


def kernel(
    shards, heads, vertical_ref, slash_ref, q_ref, k_ref, v_ref, w_hbm, out_ref,
    qt, acc, top, total, send, recv, vert_k, vert_v, weight, att, part, part_in,
    send_sem, recv_sem, vs_send, vs_recv, w_sem, h_send, h_recv,
):
    groups = qt.shape[0]
    rounds, block = k_ref.shape[0], k_ref.shape[1]
    per = q_ref.shape[1] // (groups * HD)
    width = out_ref.shape[1]
    tile = part.shape[3]
    tiles = width // tile
    verticals, slashes = vertical_ref.shape[1], slash_ref.shape[1]
    last_base = (rounds - 1) * shards
    me = lax.axis_index("ctx")
    head = lax.axis_index("head")
    steps = shards.bit_length() - 1
    bits_k, bits_v = gather_bits(shards, False), gather_bits(shards, True)
    ends = [1 + max(1, round((shards - 1) * ((step + 1) / steps) ** PACE)) for step in range(steps)]

    barrier = pltpu.get_barrier_semaphore()
    for offset in range(1, shards):
        pl.semaphore_signal(
            barrier, inc=1, device_id=(flipped(shards, me, offset), head), device_id_type=MESH
        )
    for offset in range(1, heads):
        pl.semaphore_signal(
            barrier, inc=1, device_id=(me, lax.rem(head + offset, heads)), device_id_type=MESH
        )

    def slash_of(group, residue):
        chosen = 0
        for at in range(slashes):
            offset = slash_ref[group, at]
            chosen = chosen + jnp.where(offset % shards == residue, offset, 0)
        return chosen

    def slash_bias(group, place):
        source = flipped(shards, me, send_offset(shards, place))
        chosen = slash_of(group, (me - source + shards) % shards)
        repeated = chosen == 0
        for at in range(verticals):
            repeated = repeated | (vertical_ref[group, at] == last_base + me - chosen)
        return jnp.where(repeated, NEGATIVE, 0.0)

    def vertical_place(group, at, bits):
        source = vertical_ref[group, at] % shards
        place = 0
        for step, bit in enumerate(bits):
            place = place + (1 << step) * ((source // bit + me // bit) % 2)
        return place

    def gather_copy(step, which):
        buffer = (vert_k, vert_v)[which]
        bit = (bits_k, bits_v)[which][step]
        size = 1 << step
        return pltpu.make_async_remote_copy(
            src_ref=buffer.at[pl.ds(0, size)],
            dst_ref=buffer.at[pl.ds(size, size)],
            send_sem=vs_send.at[step, which],
            recv_sem=vs_recv.at[step, which],
            device_id=(flipped(shards, me, bit), head),
            device_id_type=MESH,
        )

    def slash_copy(place):
        return pltpu.make_async_remote_copy(
            src_ref=send.at[place],
            dst_ref=recv.at[place],
            send_sem=send_sem.at[place],
            recv_sem=recv_sem.at[place],
            device_id=(flipped(shards, me, send_offset(shards, place)), head),
            device_id_type=MESH,
        )

    def fill(buffer, place):
        target = flipped(shards, me, send_offset(shards, place))
        for group in range(groups):
            chosen = slash_of(group, (target - me + shards) % shards)
            at = (last_base + target - chosen) // shards
            columns = slice(group * HD, (group + 1) * HD)
            buffer[place, group, 0] = k_ref[at, :, columns]
            buffer[place, group, 1] = v_ref[at, :, columns]

    for group in range(groups):
        at = 0
        for one in range(verticals):
            block_at = vertical_ref[group, one]
            at = at + jnp.where(block_at % shards == me, block_at // shards, 0)
        columns = slice(group * HD, (group + 1) * HD)
        vert_k[0, group] = k_ref[at, :, columns]
        vert_v[0, group] = v_ref[at, :, columns]

    pl.semaphore_wait(barrier, shards - 1 + heads - 1)
    for which in range(2):
        gather_copy(0, which).start()

    def launch(place, carry):
        fill(send, place)
        slash_copy(place).start()
        return carry

    lax.fori_loop(1, ends[0], launch, 0)
    w_copy = pltpu.make_async_copy(w_hbm, weight, w_sem)
    w_copy.start()
    fill(recv, 0)

    for group in range(groups):
        for one in range(per):
            start = (group * per + one) * HD
            rows = q_ref[:, start : start + HD].astype(jnp.float32)
            qt[group, :, one * block : (one + 1) * block] = rows.T.astype(jnp.bfloat16)

    columns_q = per * block
    causal = (
        lax.broadcasted_iota(jnp.int32, (block, columns_q), 0)
        <= lax.broadcasted_iota(jnp.int32, (block, columns_q), 1) % block
    )

    def weigh(values_tile, weights):
        return lax.dot_general(
            values_tile,
            weights.astype(jnp.bfloat16),
            (((0,), (0,)), ((), ())),
            preferred_element_type=jnp.float32,
        )

    for group in range(groups):
        columns = slice(group * HD, (group + 1) * HD)
        scores = (
            jnp.dot(
                k_ref[rounds - 1, :, columns], qt[group], preferred_element_type=jnp.float32
            )
            * SCALE
        )
        scores = jnp.where(causal, scores, NEGATIVE)
        peak = jnp.max(scores, axis=0, keepdims=True)
        weights = jnp.exp2(scores - peak)
        top[group] = peak
        total[group] = jnp.sum(weights, axis=0, keepdims=True)
        acc[group] = weigh(v_ref[rounds - 1, :, columns], weights)

    def absorb(group, keys_tile, values_tile, bias):
        scores = jnp.dot(keys_tile, qt[group], preferred_element_type=jnp.float32) * SCALE
        if bias is not None:
            scores = scores + bias
        before = top[group]
        peak = jnp.maximum(before, jnp.max(scores, axis=0, keepdims=True))
        weights = jnp.exp2(scores - peak)
        shrink = jnp.exp2(before - peak)
        top[group] = peak
        total[group] = total[group] * shrink + jnp.sum(weights, axis=0, keepdims=True)
        acc[group] = acc[group] * shrink + weigh(values_tile, weights)

    def absorb_slash(place):
        for group in range(groups):
            absorb(group, recv[place, group, 0], recv[place, group, 1], slash_bias(group, place))

    def absorb_vertical(turn, carry):
        for group in range(groups):
            keys_tile, values_tile = [], []
            for one in range(TOGETHER):
                at = turn * TOGETHER + one
                keys_tile.append(vert_k[vertical_place(group, at, bits_k), group])
                values_tile.append(vert_v[vertical_place(group, at, bits_v), group])
            absorb(group, jnp.concatenate(keys_tile), jnp.concatenate(values_tile), None)
        return carry

    def slash_arrival(place, carry):
        slash_copy(place).wait_recv()
        absorb_slash(place)
        return carry

    absorb_slash(0)
    done = 1
    for step in range(steps):
        for which in range(2):
            gather_copy(step, which).wait_recv()
        if step < steps - 1:
            for which in range(2):
                gather_copy(step + 1, which).start()
            lax.fori_loop(ends[step], ends[step + 1], launch, 0)
        if 1 <= step < steps - 1:
            lax.fori_loop(done, ends[step - 1], slash_arrival, 0)
            done = ends[step - 1]
    lax.fori_loop(0, verticals // TOGETHER, absorb_vertical, 0)
    lax.fori_loop(done, shards, slash_arrival, 0)

    for group in range(groups):
        for one in range(per):
            columns = slice(one * block, (one + 1) * block)
            scaled = acc[group, :, columns] / total[group, :, columns]
            start = (group * per + one) * HD
            att[:, start : start + HD] = scaled.T.astype(jnp.bfloat16)
    w_copy.wait()

    def project(owner, at):
        start = pl.multiple_of(owner * width + at * tile, tile)
        return jnp.dot(
            att[...], weight[:, pl.ds(start, tile)], preferred_element_type=jnp.float32
        )

    def head_copy(offset, at):
        return pltpu.make_async_remote_copy(
            src_ref=part.at[offset - 1, at],
            dst_ref=part_in.at[offset - 1, at],
            send_sem=h_send.at[offset - 1, at],
            recv_sem=h_recv.at[offset - 1, at],
            device_id=(me, lax.rem(head + offset, heads)),
            device_id_type=MESH,
        )

    for offset in range(1, heads):

        def give(at, carry, offset=offset):
            part[offset - 1, at] = project(lax.rem(head + offset, heads), at).astype(jnp.bfloat16)
            head_copy(offset, at).start()
            return carry

        lax.fori_loop(0, tiles, give, 0)

    def keep(at, carry):
        result = project(head, at)
        for offset in range(1, heads):
            head_copy(offset, at).wait_recv()
            result = result + part_in[offset - 1, at].astype(jnp.float32)
        start = pl.multiple_of(at * tile, tile)
        out_ref[:, pl.ds(start, tile)] = result.astype(jnp.bfloat16)
        return carry

    lax.fori_loop(0, tiles, keep, 0)

    for step in range(steps):
        for which in range(2):
            gather_copy(step, which).wait_send()

    def sent(place, carry):
        slash_copy(place).wait_send()
        return carry

    lax.fori_loop(1, shards, sent, 0)
    for offset in range(1, heads):
        for at in range(tiles):
            head_copy(offset, at).wait_send()


def per_device(shards, heads, queries, keys, values, out_weight, vertical, slash):
    groups = vertical.shape[0]
    block = queries.shape[0]
    per = H // KVH
    width = out_weight.shape[1] // heads
    tile = min(512, width)
    steps = shards.bit_length() - 1
    smem = pl.BlockSpec(memory_space=pltpu.SMEM)
    vmem = pl.BlockSpec(memory_space=pltpu.VMEM)
    dma = pltpu.SemaphoreType.DMA
    return pl.pallas_call(
        functools.partial(kernel, shards, heads),
        out_shape=jax.ShapeDtypeStruct((block, width), jnp.bfloat16),
        in_specs=[smem, smem, vmem, vmem, vmem, pl.BlockSpec(memory_space=pl.ANY)],
        out_specs=vmem,
        scratch_shapes=[
            pltpu.VMEM((groups, HD, per * block), jnp.bfloat16),
            pltpu.VMEM((groups, HD, per * block), jnp.float32),
            pltpu.VMEM((groups, 1, per * block), jnp.float32),
            pltpu.VMEM((groups, 1, per * block), jnp.float32),
            pltpu.VMEM((shards, groups, 2, block, HD), jnp.bfloat16),
            pltpu.VMEM((shards, groups, 2, block, HD), jnp.bfloat16),
            pltpu.VMEM((shards, groups, block, HD), jnp.bfloat16),
            pltpu.VMEM((shards, groups, block, HD), jnp.bfloat16),
            pltpu.VMEM(out_weight.shape, jnp.bfloat16),
            pltpu.VMEM((block, groups * per * HD), jnp.bfloat16),
            pltpu.VMEM((heads - 1, width // tile, block, tile), jnp.bfloat16),
            pltpu.VMEM((heads - 1, width // tile, block, tile), jnp.bfloat16),
            dma((shards,)),
            dma((shards,)),
            dma((steps, 2)),
            dma((steps, 2)),
            dma,
            dma((heads - 1, width // tile)),
            dma((heads - 1, width // tile)),
        ],
        compiler_params=pltpu.CompilerParams(
            collective_id=0, has_side_effects=True, vmem_limit_bytes=56 * 1024 * 1024
        ),
    )(vertical, slash, queries, keys, values, out_weight)


def solution(mesh):
    in_specs = (
        P("ctx", "head"),
        P(None, "ctx", "head"),
        P(None, "ctx", "head"),
        P("head", None),
        P("head", None),
        P("head", None),
    )
    return jax.shard_map(
        functools.partial(per_device, mesh.shape["ctx"], mesh.shape["head"]),
        mesh=mesh,
        in_specs=in_specs,
        out_specs=P("ctx", "head"),
        check_vma=False,
    )
```

```python
import functools
import math

import jax
import jax.numpy as jnp
from jax import lax
from jax.experimental import pallas as pl
from jax.experimental.pallas import tpu as pltpu
from jax.sharding import PartitionSpec as P

H = 32
KVH = 8
HD = 128
NEGATIVE = -1e30
SCALE = HD ** (-0.5) * math.log2(math.e)
MESH = pl.DeviceIdType.MESH


PACE = 1.5
AHEAD = 5
TOGETHER = 2


def send_offset(shards, place):
    return place // 2 + (place % 2) * (shards // 2)


def gather_bits(shards, swap):
    bits = [1 << place for place in reversed(range(shards.bit_length() - 1))]
    if swap:
        bits[-1], bits[-2] = bits[-2], bits[-1]
    return bits


def flipped(shards, index, offset):
    result = index
    for bit in (1 << place for place in range(shards.bit_length() - 1)):
        result = result + bit * ((offset // bit) % 2) * (1 - 2 * ((index // bit) % 2))
    return result


def kernel(
    shards, heads, vertical_ref, slash_ref, q_ref, k_ref, v_ref, w_hbm, out_ref,
    qt, acc, top, total, send, recv, vert_k, vert_v, weight, att, part, part_in,
    send_sem, recv_sem, vs_send, vs_recv, w_sem, h_send, h_recv,
):
    groups = qt.shape[0]
    rounds, block = k_ref.shape[0], k_ref.shape[1]
    per = q_ref.shape[1] // (groups * HD)
    width = out_ref.shape[1]
    tile = part.shape[3]
    tiles = width // tile
    verticals, slashes = vertical_ref.shape[1], slash_ref.shape[1]
    last_base = (rounds - 1) * shards
    me = lax.axis_index("ctx")
    head = lax.axis_index("head")
    steps = shards.bit_length() - 1
    bits_k, bits_v = gather_bits(shards, False), gather_bits(shards, True)
    ends = [1 + max(1, round((shards - 1) * ((step + 1) / steps) ** PACE)) for step in range(steps)]

    barrier = pltpu.get_barrier_semaphore()
    for offset in range(1, shards):
        pl.semaphore_signal(
            barrier, inc=1, device_id=(flipped(shards, me, offset), head), device_id_type=MESH
        )
    for offset in range(1, heads):
        pl.semaphore_signal(
            barrier, inc=1, device_id=(me, lax.rem(head + offset, heads)), device_id_type=MESH
        )

    def slash_of(group, residue):
        chosen = 0
        for at in range(slashes):
            offset = slash_ref[group, at]
            chosen = chosen + jnp.where(offset % shards == residue, offset, 0)
        return chosen

    def slash_bias(group, place):
        source = flipped(shards, me, send_offset(shards, place))
        chosen = slash_of(group, (me - source + shards) % shards)
        repeated = chosen == 0
        for at in range(verticals):
            repeated = repeated | (vertical_ref[group, at] == last_base + me - chosen)
        return jnp.where(repeated, NEGATIVE, 0.0)

    def vertical_place(group, at, bits):
        source = vertical_ref[group, at] % shards
        place = 0
        for step, bit in enumerate(bits):
            place = place + (1 << step) * ((source // bit + me // bit) % 2)
        return place

    def gather_copy(step, which):
        buffer = (vert_k, vert_v)[which]
        bit = (bits_k, bits_v)[which][step]
        size = 1 << step
        return pltpu.make_async_remote_copy(
            src_ref=buffer.at[pl.ds(0, size)],
            dst_ref=buffer.at[pl.ds(size, size)],
            send_sem=vs_send.at[step, which],
            recv_sem=vs_recv.at[step, which],
            device_id=(flipped(shards, me, bit), head),
            device_id_type=MESH,
        )

    def slash_copy(place):
        return pltpu.make_async_remote_copy(
            src_ref=send.at[place],
            dst_ref=recv.at[place],
            send_sem=send_sem.at[place],
            recv_sem=recv_sem.at[place],
            device_id=(flipped(shards, me, send_offset(shards, place)), head),
            device_id_type=MESH,
        )

    def fill(buffer, place):
        target = flipped(shards, me, send_offset(shards, place))
        for group in range(groups):
            chosen = slash_of(group, (target - me + shards) % shards)
            at = (last_base + target - chosen) // shards
            columns = slice(group * HD, (group + 1) * HD)
            buffer[place, group, 0] = k_ref[at, :, columns]
            buffer[place, group, 1] = v_ref[at, :, columns]

    for group in range(groups):
        at = 0
        for one in range(verticals):
            block_at = vertical_ref[group, one]
            at = at + jnp.where(block_at % shards == me, block_at // shards, 0)
        columns = slice(group * HD, (group + 1) * HD)
        vert_k[0, group] = k_ref[at, :, columns]
        vert_v[0, group] = v_ref[at, :, columns]

    pl.semaphore_wait(barrier, shards - 1 + heads - 1)
    for which in range(2):
        gather_copy(0, which).start()

    def launch(place, carry):
        fill(send, place)
        slash_copy(place).start()
        return carry

    lax.fori_loop(1, ends[0], launch, 0)
    w_copy = pltpu.make_async_copy(w_hbm, weight, w_sem)
    w_copy.start()
    fill(recv, 0)

    for group in range(groups):
        for one in range(per):
            start = (group * per + one) * HD
            rows = q_ref[:, start : start + HD].astype(jnp.float32)
            qt[group, :, one * block : (one + 1) * block] = rows.T.astype(jnp.bfloat16)

    columns_q = per * block
    causal = (
        lax.broadcasted_iota(jnp.int32, (block, columns_q), 0)
        <= lax.broadcasted_iota(jnp.int32, (block, columns_q), 1) % block
    )

    def weigh(values_tile, weights):
        return lax.dot_general(
            values_tile,
            weights.astype(jnp.bfloat16),
            (((0,), (0,)), ((), ())),
            preferred_element_type=jnp.float32,
        )

    for group in range(groups):
        columns = slice(group * HD, (group + 1) * HD)
        scores = (
            jnp.dot(
                k_ref[rounds - 1, :, columns], qt[group], preferred_element_type=jnp.float32
            )
            * SCALE
        )
        scores = jnp.where(causal, scores, NEGATIVE)
        peak = jnp.max(scores, axis=0, keepdims=True)
        weights = jnp.exp2(scores - peak)
        top[group] = peak
        total[group] = jnp.sum(weights, axis=0, keepdims=True)
        acc[group] = weigh(v_ref[rounds - 1, :, columns], weights)

    def absorb(group, keys_tile, values_tile, bias):
        scores = jnp.dot(keys_tile, qt[group], preferred_element_type=jnp.float32) * SCALE
        if bias is not None:
            scores = scores + bias
        before = top[group]
        peak = jnp.maximum(before, jnp.max(scores, axis=0, keepdims=True))
        weights = jnp.exp2(scores - peak)
        shrink = jnp.exp2(before - peak)
        top[group] = peak
        total[group] = total[group] * shrink + jnp.sum(weights, axis=0, keepdims=True)
        acc[group] = acc[group] * shrink + weigh(values_tile, weights)

    def absorb_slash(place):
        for group in range(groups):
            absorb(group, recv[place, group, 0], recv[place, group, 1], slash_bias(group, place))

    def absorb_vertical(turn, carry):
        for group in range(groups):
            keys_tile, values_tile = [], []
            for one in range(TOGETHER):
                at = turn * TOGETHER + one
                keys_tile.append(vert_k[vertical_place(group, at, bits_k), group])
                values_tile.append(vert_v[vertical_place(group, at, bits_v), group])
            absorb(group, jnp.concatenate(keys_tile), jnp.concatenate(values_tile), None)
        return carry

    def slash_arrival(place, carry):
        slash_copy(place).wait_recv()
        absorb_slash(place)
        return carry

    absorb_slash(0)
    done = 1
    for step in range(steps):
        for which in range(2):
            gather_copy(step, which).wait_recv()
        if step < steps - 1:
            for which in range(2):
                gather_copy(step + 1, which).start()
            upto = min(ends[step + 1], ends[steps - 2] + 1)
            lax.fori_loop(ends[step], upto, launch, 0)
        if 1 <= step < steps - 1:
            lax.fori_loop(done, ends[step - 1], slash_arrival, 0)
            done = ends[step - 1]
    lax.fori_loop(0, verticals // TOGETHER, absorb_vertical, 0)
    ahead = max(AHEAD, upto - done)

    def slash_turn(place, carry):
        slash_copy(place).wait_recv()
        launch(place + ahead, carry)
        absorb_slash(place)
        return carry

    lax.fori_loop(upto, done + ahead, launch, 0)
    lax.fori_loop(done, shards - ahead, slash_turn, 0)
    lax.fori_loop(shards - ahead, shards, slash_arrival, 0)

    for group in range(groups):
        for one in range(per):
            columns = slice(one * block, (one + 1) * block)
            scaled = acc[group, :, columns] / total[group, :, columns]
            start = (group * per + one) * HD
            att[:, start : start + HD] = scaled.T.astype(jnp.bfloat16)
    w_copy.wait()

    def project(owner, at):
        start = pl.multiple_of(owner * width + at * tile, tile)
        return jnp.dot(
            att[...], weight[:, pl.ds(start, tile)], preferred_element_type=jnp.float32
        )

    def head_copy(offset, at):
        return pltpu.make_async_remote_copy(
            src_ref=part.at[offset - 1, at],
            dst_ref=part_in.at[offset - 1, at],
            send_sem=h_send.at[offset - 1, at],
            recv_sem=h_recv.at[offset - 1, at],
            device_id=(me, lax.rem(head + offset, heads)),
            device_id_type=MESH,
        )

    for offset in range(1, heads):

        def give(at, carry, offset=offset):
            part[offset - 1, at] = project(lax.rem(head + offset, heads), at).astype(jnp.bfloat16)
            head_copy(offset, at).start()
            return carry

        lax.fori_loop(0, tiles, give, 0)

    def keep(at, carry):
        result = project(head, at)
        for offset in range(1, heads):
            head_copy(offset, at).wait_recv()
            result = result + part_in[offset - 1, at].astype(jnp.float32)
        start = pl.multiple_of(at * tile, tile)
        out_ref[:, pl.ds(start, tile)] = result.astype(jnp.bfloat16)
        return carry

    lax.fori_loop(0, tiles, keep, 0)

    for step in range(steps):
        for which in range(2):
            gather_copy(step, which).wait_send()

    def sent(place, carry):
        slash_copy(place).wait_send()
        return carry

    lax.fori_loop(1, shards, sent, 0)
    for offset in range(1, heads):
        for at in range(tiles):
            head_copy(offset, at).wait_send()


def per_device(shards, heads, queries, keys, values, out_weight, vertical, slash):
    groups = vertical.shape[0]
    block = queries.shape[0]
    per = H // KVH
    width = out_weight.shape[1] // heads
    tile = min(512, width)
    steps = shards.bit_length() - 1
    smem = pl.BlockSpec(memory_space=pltpu.SMEM)
    vmem = pl.BlockSpec(memory_space=pltpu.VMEM)
    dma = pltpu.SemaphoreType.DMA
    return pl.pallas_call(
        functools.partial(kernel, shards, heads),
        out_shape=jax.ShapeDtypeStruct((block, width), jnp.bfloat16),
        in_specs=[smem, smem, vmem, vmem, vmem, pl.BlockSpec(memory_space=pl.ANY)],
        out_specs=vmem,
        scratch_shapes=[
            pltpu.VMEM((groups, HD, per * block), jnp.bfloat16),
            pltpu.VMEM((groups, HD, per * block), jnp.float32),
            pltpu.VMEM((groups, 1, per * block), jnp.float32),
            pltpu.VMEM((groups, 1, per * block), jnp.float32),
            pltpu.VMEM((shards, groups, 2, block, HD), jnp.bfloat16),
            pltpu.VMEM((shards, groups, 2, block, HD), jnp.bfloat16),
            pltpu.VMEM((shards, groups, block, HD), jnp.bfloat16),
            pltpu.VMEM((shards, groups, block, HD), jnp.bfloat16),
            pltpu.VMEM(out_weight.shape, jnp.bfloat16),
            pltpu.VMEM((block, groups * per * HD), jnp.bfloat16),
            pltpu.VMEM((heads - 1, width // tile, block, tile), jnp.bfloat16),
            pltpu.VMEM((heads - 1, width // tile, block, tile), jnp.bfloat16),
            dma((shards,)),
            dma((shards,)),
            dma((steps, 2)),
            dma((steps, 2)),
            dma,
            dma((heads - 1, width // tile)),
            dma((heads - 1, width // tile)),
        ],
        compiler_params=pltpu.CompilerParams(
            collective_id=0, has_side_effects=True, vmem_limit_bytes=56 * 1024 * 1024
        ),
    )(vertical, slash, queries, keys, values, out_weight)


def solution(mesh):
    in_specs = (
        P("ctx", "head"),
        P(None, "ctx", "head"),
        P(None, "ctx", "head"),
        P("head", None),
        P("head", None),
        P("head", None),
    )
    return jax.shard_map(
        functools.partial(per_device, mesh.shape["ctx"], mesh.shape["head"]),
        mesh=mesh,
        in_specs=in_specs,
        out_specs=P("ctx", "head"),
        check_vma=False,
    )
```
